32 devices in a mesh: blk: 2 (over core), row: 16 (over z, y, x).
Axes of the slice: x: 2, y: 2, z: 4, core: 2. Of those that a mesh axis runs over, the one named last changes fastest.
Arguments:
- queries: bfloat16 [16, 16, 8192], P('row', None, 'blk')
- new_keys: bfloat16 [16, 16, 1024], P('row', None, 'blk')
- new_values: bfloat16 [16, 16, 1024], P('row', None, 'blk'), may hold values from -6 to 6
- cache_keys: bfloat16 [16, 1024, 1024], P('row', 'blk')
- cache_values: bfloat16 [16, 1024, 1024], P('row', 'blk'), may hold values from -6 to 6
- lengths: int32 [16], replicated, may hold values from 1 to 1024, as said below
- resid: bfloat16 [16, 16, 5120], P('row', 'blk'), may hold values from -6 to 6
- out_proj: bfloat16 [8192, 5120], P('blk'), may hold values from -0.0625 to 0.0625
- norm_gain: float32 [5120], replicated, may hold values from 0.1 to 1.9
- w_gate: bfloat16 [16, 5120, 3200], P('row', None, 'blk'), may hold values from -0.078125 to 0.078125
- w_up: bfloat16 [16, 5120, 3200], P('row', None, 'blk'), may hold values from -0.078125 to 0.078125
- w_down: bfloat16 [16, 3200, 5120], P('row', 'blk'), may hold values from -0.0546875 to 0.0546875
Outputs:
- attended: bfloat16 [16, 16, 5120], P('row', 'blk')
- layer_out: bfloat16 [16, 16, 5120], P('row', 'blk')
The draws below stay inside these ranges and needn't reach their ends.
Inputs may be any that keep to these rules, and one draw needn't show every extreme that they name: `lengths`: entries of rows 12 and above are not read; some row has all 1024 positions cached.
All inputs are finite; a program needn't handle non-finite values.
Results may differ from the reference program's by a relative error of at most 0.0044.
Values may be sent and summed in bfloat16 or wider, within the bound.
A program may use at most 256 MiB of HBM per device.

```python
import math
import jax
import jax.numpy as jnp
from jax import lax

D = 5120
HEADS = 64
KV = 8
HD = 128
FF = 12800
TURN = 16
C = 512
GROUP = 8
N_FR = 4
N_AR = 12
CACHE = 1024
FFQ = 3200
N_BLK = 2
N_ROW = 16


def draw_queries(key, part):
    key = jax.random.fold_in(key, 11)
    shape = (N_ROW, TURN, HEADS * HD)
    return jax.random.normal(key, shape, jnp.float32).astype(jnp.bfloat16)


def draw_new_keys(key, part):
    key = jax.random.fold_in(key, 12)
    shape = (N_ROW, TURN, KV * HD)
    return jax.random.normal(key, shape, jnp.float32).astype(jnp.bfloat16)


def draw_cache_keys(key, part):
    key = jax.random.fold_in(key, 13)
    shape = (N_ROW, CACHE, KV * HD)
    return jax.random.normal(key, shape, jnp.float32).astype(jnp.bfloat16)


def draw_lengths(key, part):
    key = jax.random.fold_in(key, 14)
    drawn = jax.random.randint(key, (N_ROW,), 1, CACHE + 1, jnp.int32)
    return drawn.at[0].set(CACHE)


def levels(key, extent, pieces, least, high):
    def one(dim, parts):
        draws = jax.random.uniform(jax.random.fold_in(jax.random.fold_in(key, 6), dim), (parts,), jnp.float32, least / len(pieces), high / len(pieces))
        return jnp.repeat(jnp.exp(draws), extent[dim] // parts).reshape((-1,) + (1,) * (len(extent) - dim - 1))

    level = one(*pieces[0])
    for cut in pieces[1:]:
        level = level * one(*cut)
    return level


def noise(key, extent, scale, limit, cuts=(), dtype=jnp.bfloat16):
    values = jax.random.normal(key, extent, jnp.float32) * scale
    if len(cuts) > 0:
        values = levels(key, extent, cuts, -0.22, 0.18) * values
    return jnp.clip(values, min=-limit, max=limit).astype(dtype)


def setup_inputs(seed: int = 0) -> dict:
    keys = jax.random.split(jax.random.key(seed), 13)
    return {
        "queries": draw_queries(jax.random.fold_in(keys[12], 71), 0),
        "new_keys": draw_new_keys(jax.random.fold_in(keys[12], 71), 0),
        "new_values": noise(keys[2], (N_ROW, TURN, KV * HD), 1.0, 6.0, ((0, 16), (2, 2))),
        "cache_keys": draw_cache_keys(jax.random.fold_in(keys[12], 71), 0),
        "cache_values": noise(keys[4], (N_ROW, CACHE, KV * HD), 1.0, 6.0, ((0, 16), (1, 2))),
        "lengths": draw_lengths(jax.random.fold_in(keys[12], 71), 0),
        "resid": noise(keys[6], (N_ROW, TURN, D), 1.0, 6.0, ((0, 16), (1, 2))),
        "out_proj": noise(keys[7], (HEADS * HD, D), (HEADS * HD) ** -0.5, 0.0625, ((0, 2),)),
        "norm_gain": jnp.clip(1.0 + 0.18 * jax.random.normal(keys[8], (D,), jnp.float32), 0.1, 1.9),
        "w_gate": noise(keys[9], (N_ROW, D, FFQ), D ** -0.5, 0.078125, ((0, 16), (2, 2))),
        "w_up": noise(keys[10], (N_ROW, D, FFQ), D ** -0.5, 0.078125, ((0, 16), (2, 2))),
        "w_down": noise(keys[11], (N_ROW, FFQ, D), FF ** -0.5, 0.0546875, ((0, 16), (1, 2))),
    }


def block_partial(query_block, key_block, value_block, allowed):
    scale = 1.0 / math.sqrt(query_block.shape[-1])
    scores = jnp.einsum('tkgd,pkd->tkgp', query_block.astype(jnp.float32), key_block.astype(jnp.float32)) * scale
    mask = allowed[:, None, None, :]
    peak = lax.optimization_barrier(jnp.max(jnp.where(mask, scores, -1e+30), axis=-1))
    weights = jnp.where(mask, jnp.exp(scores - peak[..., None]), 0.0)
    totals = lax.optimization_barrier(jnp.sum(weights, axis=-1))
    probs = lax.optimization_barrier(weights.astype(jnp.bfloat16)).astype(jnp.float32)
    summed = jnp.einsum('tkgp,pkd->tkgd', probs, value_block.astype(jnp.float32))
    safe = jnp.maximum(totals, 1.0)
    return (summed / safe[..., None], peak + jnp.log(safe))

def attend_row(packed):
    query_row, key_row, value_row, cache_k, cache_v, length = packed
    query_heads = query_row.reshape(TURN, KV, GROUP, HD)
    steps_idx = jnp.arange(TURN)
    turn_mask = steps_idx[None, :] <= steps_idx[:, None]
    out_turn, lse_turn = block_partial(query_heads, key_row.reshape(TURN, KV, HD), value_row.reshape(TURN, KV, HD), turn_mask)
    outputs = [out_turn]
    lses = [lse_turn]
    for shard in range(N_BLK):
        positions = shard * C + jnp.arange(C)
        allowed = jnp.broadcast_to((positions < length)[None, :], (TURN, C))
        keys_part = cache_k[shard * C:(shard + 1) * C].reshape(C, KV, HD)
        values_part = cache_v[shard * C:(shard + 1) * C].reshape(C, KV, HD)
        out_b, lse_b = block_partial(query_heads, keys_part, values_part, allowed)
        outputs.append(out_b)
        lses.append(lse_b)
    stacked_out = jnp.stack(outputs)
    stacked_lse = jnp.stack(lses)
    largest = lax.optimization_barrier(jnp.max(stacked_lse, axis=0))
    factors = jnp.exp(stacked_lse - largest[None])
    combined = lax.optimization_barrier(jnp.sum(factors[..., None] * stacked_out, axis=0)) / lax.optimization_barrier(jnp.sum(factors, axis=0))[..., None]
    return combined.reshape(TURN, HEADS * HD).astype(jnp.bfloat16)

def reference(queries, new_keys, new_values, cache_keys, cache_values, lengths, resid, out_proj, norm_gain, w_gate, w_up, w_down):
    attn_rows = lax.map(attend_row, (queries[:N_AR], new_keys[:N_AR], new_values[:N_AR], cache_keys[:N_AR], cache_values[:N_AR], lengths[:N_AR]))
    projected = jnp.dot(attn_rows.reshape(N_AR * TURN, HEADS * HD), out_proj, preferred_element_type=jnp.float32)
    mid = resid[:N_AR].reshape(N_AR * TURN, D).astype(jnp.float32) + projected
    normed = (mid * lax.rsqrt(lax.optimization_barrier(jnp.mean(mid * mid, axis=-1, keepdims=True)) + 1e-06) * norm_gain).astype(jnp.bfloat16)
    gate_full = jnp.moveaxis(w_gate[N_AR:], 0, 1).reshape(D, FF)
    up_full = jnp.moveaxis(w_up[N_AR:], 0, 1).reshape(D, FF)
    down_full = w_down[N_AR:].reshape(FF, D)
    gate = jnp.dot(normed, gate_full, preferred_element_type=jnp.float32)
    upper = jnp.dot(normed, up_full, preferred_element_type=jnp.float32)
    hidden = (jax.nn.silu(gate) * upper).astype(jnp.bfloat16)
    ffn = jnp.dot(hidden, down_full, preferred_element_type=jnp.float32)
    blank = jnp.zeros((N_FR, TURN, D), jnp.bfloat16)
    attended = jnp.concatenate([mid.astype(jnp.bfloat16).reshape(N_AR, TURN, D), blank], axis=0)
    layer_out = jnp.concatenate([(mid + ffn).astype(jnp.bfloat16).reshape(N_AR, TURN, D), blank], axis=0)
    return (attended, layer_out)
```

```python
import functools
import math

import jax
import jax.numpy as jnp
from jax import lax
from jax.experimental import pallas as pl
from jax.experimental.pallas import tpu as pltpu
from jax.sharding import PartitionSpec as P

HD = 128
GROUP = 8
MESH = pl.DeviceIdType.MESH
F32 = jnp.float32
BF16 = jnp.bfloat16
TILE = 256
SPAN = 512
DEPTH = 512


def contract_last(a, b):
    return lax.dot_general(a, b, (((1,), (1,)), ((), ())), preferred_element_type=F32)


def kernel(
    n_row, n_slot,
    lengths, queries, new_keys, new_values, cache_keys, cache_values, resid, out_proj, gain,
    w_gate, w_up, w_down,
    attended, layer_out,
    k_far, v_far, acc, acc_far, normed, tokens, ffn_in,
    core_out, core_in, plane_out, plane_in, final,
    kv_send, kv_recv, acc_sems, norm_send, tok_recv, tok_send, relay_send, relay_recv,
    core_send, core_recv, plane_send, plane_recv, final_send, ffn_recv, mate_send, mate_recv,
):
    blk = lax.axis_index("blk")
    row = lax.axis_index("row")
    mate = 1 - blk
    n_ffn = n_row // 4
    n_att = n_row - n_ffn
    per = n_att // n_ffn
    turn = queries.shape[1]
    width = out_proj.shape[1]
    half = width // 2
    n_piece = half // SPAN
    local = new_keys.shape[2]
    kv_here = local // HD
    shard = cache_keys.shape[1]
    n_chunk = out_proj.shape[0] // DEPTH
    units = w_gate.shape[1]
    sibling = {"blk": mate, "row": row}
    my_cols = pl.ds(pl.multiple_of(blk * half, 128), half)
    mate_cols = pl.ds(pl.multiple_of(mate * half, 128), half)
    barrier = pltpu.get_barrier_semaphore()

    def remote(src, dst, send, recv, device):
        return pltpu.make_async_remote_copy(
            src_ref=src, dst_ref=dst, send_sem=send, recv_sem=recv,
            device_id=device, device_id_type=MESH,
        )

    def greet(device):
        pl.semaphore_signal(barrier, inc=1, device_id=device, device_id_type=MESH)

    def attention(wo_buf, k_own, v_own, attn, mid, wo_sem, own_sem):
        column = lax.rem(row, n_ffn)
        place = lax.div(row, n_ffn)
        server = {"blk": blk, "row": n_att + column}
        greet(sibling)
        greet(server)
        own_heads = pl.ds(pl.multiple_of(blk * local, 128), local)
        far_heads = pl.ds(pl.multiple_of(mate * local, 128), local)
        own_k = pltpu.make_async_copy(cache_keys.at[0, :, own_heads], k_own, own_sem.at[0])
        own_v = pltpu.make_async_copy(cache_values.at[0, :, own_heads], v_own, own_sem.at[1])
        own_k.start()
        own_v.start()

        def wo_copy(s):
            slot = lax.rem(s, n_slot)
            return pltpu.make_async_copy(
                out_proj.at[pl.ds(pl.multiple_of(s * DEPTH, DEPTH), DEPTH)],
                wo_buf.at[slot], wo_sem.at[slot],
            )

        pl.semaphore_wait(barrier, 2)
        send_k = remote(
            cache_keys.at[0, :, far_heads], k_far, kv_send.at[0], kv_recv.at[0], sibling
        )
        send_v = remote(
            cache_values.at[0, :, far_heads], v_far, kv_send.at[1], kv_recv.at[1], sibling
        )
        send_k.start()
        send_v.start()

        @pl.loop(0, min(n_slot, n_chunk))
        def _(s):
            wo_copy(s).start()

        own_k.wait()
        own_v.wait()
        send_k.wait()
        send_v.wait()

        length = lengths[row]
        scale = 1.0 / math.sqrt(HD)
        rows = turn * GROUP
        turn_mask = lax.broadcasted_iota(jnp.int32, (rows, turn), 1) <= jnp.bitwise_and(
            lax.broadcasted_iota(jnp.int32, (rows, turn), 0), turn - 1
        )
        spot = lax.broadcasted_iota(jnp.int32, (rows, shard), 1)
        own_mask = spot + blk * shard < length
        far_mask = spot + mate * shard < length
        for k in range(kv_here):
            heads = slice(k * HD, (k + 1) * HD)
            query = jnp.concatenate(
                [queries[0, :, (k * GROUP + g) * HD : (k * GROUP + g + 1) * HD]
                 for g in range(GROUP)], axis=0,
            )
            parts = []
            for mask, keys in (
                (turn_mask, new_keys[0, :, heads]),
                (own_mask, k_own[:, heads]),
                (far_mask, k_far[:, heads]),
            ):
                parts.append(jnp.where(mask, contract_last(query, keys) * scale, -1e30))
            peak = functools.reduce(
                jnp.maximum, [jnp.max(s, axis=-1, keepdims=True) for s in parts]
            )
            total = jnp.zeros((rows, 1), F32)
            summed = jnp.zeros((rows, HD), F32)
            for s, mask, values in (
                (parts[0], turn_mask, new_values[0, :, heads]),
                (parts[1], own_mask, v_own[:, heads]),
                (parts[2], far_mask, v_far[:, heads]),
            ):
                weights = jnp.where(mask, jnp.exp(s - peak), 0.0)
                total += jnp.sum(weights, axis=-1, keepdims=True)
                summed += jnp.dot(weights.astype(BF16), values, preferred_element_type=F32)
            out = (summed / total).astype(BF16)
            for g in range(GROUP):
                attn[:, (k * GROUP + g) * HD : (k * GROUP + g + 1) * HD] = out[
                    g * turn : (g + 1) * turn
                ]

        acc[...] = jnp.zeros_like(acc)
        mine = pl.ds(pl.multiple_of(blk * (turn // 2), turn // 2), turn // 2)
        acc[mine, :] = resid[0].astype(F32)

        @pl.loop(0, n_chunk)
        def _(s):
            wo_copy(s).wait()
            some = attn[:, pl.ds(pl.multiple_of(s * DEPTH, DEPTH), DEPTH)]
            acc[...] += jnp.dot(some, wo_buf[lax.rem(s, n_slot)], preferred_element_type=F32)
            if n_slot < n_chunk:
                @pl.when(s + n_slot < n_chunk)
                def _():
                    wo_copy(s + n_slot).start()

        swap = remote(acc, acc_far, acc_sems.at[0], acc_sems.at[1], sibling)
        swap.start()
        swap.wait()
        value = acc[...] + acc_far[...]
        mid[...] = value
        square = jnp.mean(value * value, axis=-1, keepdims=True)
        normed[...] = (value * lax.rsqrt(square + 1e-06) * gain[...]).astype(BF16)
        spread = remote(
            normed.at[:, my_cols],
            tokens.at[pl.ds(pl.multiple_of((column * per + place) * turn, turn), turn), my_cols],
            norm_send, tok_recv.at[column * per + place], server,
        )
        spread.start()
        attended[0] = mid[mine, :].astype(BF16)

        def mate_copy(j, side):
            cols = pl.ds(pl.multiple_of(side * half + j * SPAN, 128), SPAN)
            return remote(
                ffn_in.at[:, cols], ffn_in.at[:, cols], mate_send.at[j], mate_recv.at[j], sibling
            )

        @pl.loop(0, n_piece)
        def _(j):
            cols = pl.ds(pl.multiple_of(blk * half + j * SPAN, 128), SPAN)
            remote(
                ffn_in.at[:, cols], ffn_in.at[:, cols], mate_send.at[j], ffn_recv.at[j], sibling
            ).wait_recv()
            mate_copy(j, blk).start()

        @pl.loop(0, n_piece)
        def _(j):
            mate_copy(j, mate).wait_recv()

        @pl.loop(0, n_piece)
        def _(j):
            mate_copy(j, blk).wait_send()

        acc_far[...] = ffn_in[...].astype(F32)
        layer_out[0] = (mid[mine, :] + acc_far[mine, :]).astype(BF16)
        spread.wait_send()

    def feed_forward(gate_buf, up_buf, down_buf, hidden, w_sem):
        me = row - n_att

        gate_copy = pltpu.make_async_copy(w_gate.at[0], gate_buf, w_sem.at[0])
        up_copy = pltpu.make_async_copy(w_up.at[0], up_buf, w_sem.at[1])
        down_copy = pltpu.make_async_copy(w_down.at[0], down_buf, w_sem.at[2])
        gate_copy.start()
        up_copy.start()
        down_copy.start()
        greet(sibling)
        for i in range(per):
            greet({"blk": blk, "row": me + i * n_ffn})

        def peer(step):
            return lax.rem(me + step, n_ffn)

        def at(c):
            return {"blk": blk, "row": n_att + c}

        @pl.loop(1, n_ffn)
        def _(step):
            greet(at(peer(step)))

        pl.semaphore_wait(barrier, per + n_ffn)
        attended[...] = jnp.zeros_like(attended)
        layer_out[...] = jnp.zeros_like(layer_out)

        def piece(p, cols):
            return tokens.at[pl.ds(pl.multiple_of(p * turn, turn), turn), cols]

        def forward(i, step):
            p = me * per + i
            return remote(
                piece(p, my_cols), piece(p, my_cols), tok_send.at[i, step], tok_recv.at[p],
                at(peer(step)),
            )

        def arrive(p):
            remote(
                piece(p, my_cols), piece(p, my_cols), relay_send.at[p], tok_recv.at[p], sibling
            ).wait_recv()

        def relay(p, cols):
            return remote(
                piece(p, cols), piece(p, cols), relay_send.at[p], relay_recv.at[p], sibling
            )

        for i in reversed(range(per)):
            arrive(me * per + i)

            @pl.loop(1, n_ffn)
            def _(step):
                forward(i, step).start()

            relay(me * per + i, my_cols).start()

        for i in reversed(range(per)):
            @pl.loop(1, n_ffn)
            def _(step):
                p = peer(step) * per + i
                arrive(p)
                relay(p, my_cols).start()

        @pl.loop(0, n_att)
        def _(p):
            relay(p, mate_cols).wait_recv()

        gate_copy.wait()
        up_copy.wait()

        def block(cols):
            x = tokens[...]
            g = contract_last(x, gate_buf[cols, :])
            u = contract_last(x, up_buf[cols, :])
            hidden[:, cols] = (g / (1.0 + jnp.exp(-g)) * u).astype(BF16)

        @pl.loop(0, units // TILE)
        def _(j):
            block(pl.ds(pl.multiple_of(j * TILE, TILE), TILE))

        if units % TILE:
            block(slice(units // TILE * TILE, units))

        down_copy.wait()

        def down(side, j):
            cols = pl.ds(pl.multiple_of(side * half + j * SPAN, 128), SPAN)
            return jnp.dot(hidden[...], down_buf[:, cols], preferred_element_type=F32)

        def core_copy(j):
            return remote(core_out.at[j], core_in.at[j], core_send.at[j], core_recv.at[j], sibling)

        @pl.loop(0, n_piece)
        def _(j):
            core_out[j] = down(mate, j).astype(BF16)
            core_copy(j).start()

        def group_rows(c):
            return pl.ds(pl.multiple_of(c * per * turn, turn), per * turn)

        def plane_copy(j, step):
            c = peer(step)
            return remote(
                plane_out.at[j, group_rows(c)], plane_in.at[me, j],
                plane_send.at[j, step], plane_recv.at[me, j], at(c),
            )

        @pl.loop(0, n_piece)
        def _(j):
            part = down(blk, j)
            core_copy(j).wait_recv()
            plane_out[j] = (part + core_in[j].astype(F32)).astype(BF16)

            @pl.loop(1, n_ffn)
            def _(step):
                plane_copy(j, step).start()

        def final_copy(j, i):
            cols = pl.ds(pl.multiple_of(blk * half + j * SPAN, 128), SPAN)
            return remote(
                final.at[j, pl.ds(i * turn, turn)], ffn_in.at[:, cols],
                final_send.at[j, i], ffn_recv.at[j], {"blk": blk, "row": me + i * n_ffn},
            )

        @pl.loop(0, n_piece)
        def _(j):
            def add(step, total):
                c = peer(step)
                remote(
                    plane_out.at[j, group_rows(c)], plane_in.at[c, j],
                    plane_send.at[j, step], plane_recv.at[c, j], at(c),
                ).wait_recv()
                return total + plane_in[c, j].astype(F32)

            total = plane_out[j, group_rows(me)].astype(F32)
            final[j] = lax.fori_loop(1, n_ffn, add, total).astype(BF16)
            for i in range(per):
                final_copy(j, i).start()

        @pl.loop(0, n_piece)
        def _(j):
            core_copy(j).wait_send()
            for i in range(per):
                final_copy(j, i).wait_send()

            @pl.loop(1, n_ffn)
            def _(step):
                plane_copy(j, step).wait_send()

        for i in range(per):
            @pl.loop(1, n_ffn)
            def _(step):
                forward(i, step).wait_send()

        @pl.loop(0, n_att)
        def _(p):
            relay(p, my_cols).wait_send()

    @pl.when(row < n_att)
    def _():
        pl.run_scoped(
            attention,
            pltpu.VMEM((n_slot, DEPTH, width), BF16),
            pltpu.VMEM((shard, local), BF16),
            pltpu.VMEM((shard, local), BF16),
            pltpu.VMEM((turn, out_proj.shape[0]), BF16),
            pltpu.VMEM((turn, width), F32),
            pltpu.SemaphoreType.DMA((n_slot,)),
            pltpu.SemaphoreType.DMA((2,)),
        )

    @pl.when(row >= n_att)
    def _():
        pl.run_scoped(
            feed_forward,
            pltpu.VMEM((units, width), BF16),
            pltpu.VMEM((units, width), BF16),
            pltpu.VMEM((units, width), BF16),
            pltpu.VMEM((n_att * turn, units), BF16),
            pltpu.SemaphoreType.DMA((3,)),
        )


def body(
    queries, new_keys, new_values, cache_keys, cache_values, lengths, resid, out_proj, norm_gain,
    w_gate, w_up, w_down,
):
    n_row = lax.axis_size("row")
    n_ffn = n_row // 4
    n_att = n_row - n_ffn
    per = n_att // n_ffn
    turn = queries.shape[1]
    width = out_proj.shape[1]
    half = width // 2
    n_piece = half // SPAN
    shard = cache_keys.shape[1]
    local = new_keys.shape[2]
    n_tok = n_att * turn
    n_slot = 8 if n_tok <= 256 else 4
    vmem = pl.BlockSpec(memory_space=pltpu.VMEM)
    anywhere = pl.BlockSpec(memory_space=pl.ANY)
    dma = pltpu.SemaphoreType.DMA
    out = jax.ShapeDtypeStruct(resid.shape, BF16)
    return pl.pallas_call(
        functools.partial(kernel, n_row, n_slot),
        out_shape=(out, out),
        in_specs=[
            pl.BlockSpec(memory_space=pltpu.SMEM), vmem, vmem, vmem, anywhere, anywhere, vmem,
            anywhere, vmem, anywhere, anywhere, anywhere,
        ],
        out_specs=(vmem, vmem),
        scratch_shapes=[
            pltpu.VMEM((shard, local), BF16),
            pltpu.VMEM((shard, local), BF16),
            pltpu.VMEM((turn, width), F32),
            pltpu.VMEM((turn, width), F32),
            pltpu.VMEM((turn, width), BF16),
            pltpu.VMEM((n_tok, width), BF16),
            pltpu.VMEM((turn, width), BF16),
            pltpu.VMEM((n_piece, n_tok, SPAN), BF16),
            pltpu.VMEM((n_piece, n_tok, SPAN), BF16),
            pltpu.VMEM((n_piece, n_tok, SPAN), BF16),
            pltpu.VMEM((n_ffn, n_piece, per * turn, SPAN), BF16),
            pltpu.VMEM((n_piece, per * turn, SPAN), BF16),
            dma((2,)),
            dma((2,)),
            dma((2,)),
            dma,
            dma((n_att,)),
            dma((per, n_ffn)),
            dma((n_att,)),
            dma((n_att,)),
            dma((n_piece,)),
            dma((n_piece,)),
            dma((n_piece, n_ffn)),
            dma((n_ffn, n_piece)),
            dma((n_piece, per)),
            dma((n_piece,)),
            dma((n_piece,)),
            dma((n_piece,)),
        ],
        compiler_params=pltpu.CompilerParams(
            collective_id=0, has_side_effects=True, vmem_limit_bytes=60 * 1024 * 1024,
        ),
        cost_estimate=pl.CostEstimate(
            flops=10_000_000_000, bytes_accessed=60_000_000, transcendentals=600_000
        ),
    )(
        lengths, queries, new_keys, new_values, cache_keys, cache_values, resid, out_proj,
        norm_gain.reshape(1, width), jnp.swapaxes(w_gate, 1, 2), jnp.swapaxes(w_up, 1, 2), w_down,
    )


def solution(mesh):
    placed = (
        P("row", None, "blk"),
        P("row", None, "blk"),
        P("row", None, "blk"),
        P("row", "blk", None),
        P("row", "blk", None),
        P(),
        P("row", "blk", None),
        P("blk", None),
        P(),
        P("row", None, "blk"),
        P("row", None, "blk"),
        P("row", "blk", None),
    )
    return jax.shard_map(
        body,
        mesh=mesh,
        in_specs=placed,
        out_specs=(P("row", "blk", None), P("row", "blk", None)),
        check_vma=False,
    )
```
